1024 devices in a mesh: ctx: 128 (over z_lo, y, x), tp: 8 (over z_hi, core).
Axes of the slice: x: 8, y: 8, z: 8 (z_hi: 4, z_lo: 2; z = z_hi * 2 + z_lo), core: 2. Of those that a mesh axis runs over, the one named last changes fastest.
Arguments:
- value_path: bfloat16 [16384, 8192], P('ctx', 'tp'), may hold values from -6 to 6
- key_se: bfloat16 [16384, 8192], P('ctx', 'tp'), may hold values from -6 to 6
- query_se: bfloat16 [16384, 8192], P('ctx', 'tp'), may hold values from -60 to 60
- key_mr: bfloat16 [16384, 8192], P('ctx', 'tp'), may hold values from -6 to 6
- query_mr: bfloat16 [16384, 8192], P('ctx', 'tp'), may hold values from -6 to 6
- out_grad: bfloat16 [16384, 8192], P('ctx', 'tp'), may hold values from -6 to 6
- norm_gain: bfloat16 [8192], P('tp'), may hold values from 0.099609375 to 1.8984375
- filter_se: bfloat16 [7, 8192], P(None, 'tp'), may hold values from -2 to 2
- filter_mr: bfloat16 [128, 8192], P(None, 'tp'), may hold values from -0.5 to 0.5
Outputs:
- grad_value: bfloat16 [16384, 8192], P('ctx', 'tp')
- grad_query_se: bfloat16 [16384, 8192], P('ctx', 'tp')
- grad_key_se: bfloat16 [16384, 8192], P('ctx', 'tp')
- grad_query_mr: bfloat16 [16384, 8192], P('ctx', 'tp')
- grad_key_mr: bfloat16 [16384, 8192], P('ctx', 'tp')
- grad_filter_se: float32 [7, 8192], P(None, 'tp')
- grad_filter_mr: float32 [128, 8192], P(None, 'tp')
- grad_gain: float32 [8192], P('tp')
The draws below stay inside these ranges and needn't reach their ends.
All inputs are finite; a program needn't handle non-finite values.
Results may differ from the reference program's by a relative error of at most 0.015.
Values may be sent and summed in bfloat16 or wider, within the bound.
No kernel may reach another device: no remote copies, remote signals or barrier semaphores. Data moves between devices by JAX's collectives and lax.ppermute only.
A program may use at most 32 MiB of HBM per device.

```python
import math
import jax
import jax.numpy as jnp
from jax import lax

D = 8192
SE_TAPS = 7
MR_TAPS = 128
TOKENS = 16384


def draw_query_se(key, part):
    key = jax.random.fold_in(key, 11)
    key_base, key_cols, key_rows = jax.random.split(key, 3)
    base = jnp.clip(jax.random.normal(key_base, (TOKENS, D), jnp.float32), -6.0, 6.0)
    position = jnp.arange(D, dtype=jnp.float32) / D
    cols = jnp.exp(math.log(10.0) * (0.5 * position + 0.5 * jax.random.uniform(key_cols, (D,), jnp.float32)))
    rows = jnp.exp(math.log(10.0) * jax.random.uniform(key_rows, (TOKENS, 1), jnp.float32))
    return (base * cols[None, :] * rows / 10.0).astype(jnp.bfloat16)


def shard_levels(key, shape, pieces, smallest, high):
    factor_of = 1.0
    for dim, shards_of in pieces:
        steps = jax.random.uniform(jax.random.fold_in(jax.random.fold_in(key, 6), dim), (shards_of,), jnp.float32, smallest / len(pieces), high / len(pieces))
        factor_of = factor_of * jnp.repeat(jnp.exp(steps), shape[dim] // shards_of).reshape((-1,) + (1,) * (len(shape) - 1 - dim))
    return factor_of


def noise(rng, extent, deviation, reach, cuts=(), held_as=jnp.bfloat16):
    values = jax.random.normal(rng, extent, jnp.float32) * deviation
    if len(cuts) > 0:
        values = shard_levels(rng, extent, cuts, -0.22, 0.18) * values
    return jnp.clip(values, min=-reach, max=reach).astype(held_as)


def setup_inputs(seed: int = 0) -> dict:
    keys = jax.random.split(jax.random.key(seed), 10)
    value_path = noise(keys[0], (TOKENS, D), 1.0, 6.0, ((0, 128), (1, 8)))
    key_se = noise(keys[1], (TOKENS, D), 1.0, 6.0, ((0, 128), (1, 8)))
    query_se = draw_query_se(jax.random.fold_in(keys[9], 71), 0)
    key_mr = noise(keys[3], (TOKENS, D), 1.0, 6.0, ((0, 128), (1, 8)))
    query_mr = noise(keys[4], (TOKENS, D), 1.0, 6.0, ((0, 128), (1, 8)))
    out_grad = noise(keys[5], (TOKENS, D), 1.0, 6.0, ((0, 128), (1, 8)))
    norm_gain = jnp.clip(1.0 + 0.18 * jax.random.normal(keys[6], (D,), jnp.float32), 0.099609375, 1.8984375).astype(jnp.bfloat16)
    filter_se = noise(keys[7], (SE_TAPS, D), SE_TAPS ** -0.5, 2.0, ((1, 8),))
    filter_mr = noise(keys[8], (MR_TAPS, D), MR_TAPS ** -0.5, 0.5, ((1, 8),))
    return {"value_path": value_path, "key_se": key_se, "query_se": query_se, "key_mr": key_mr, "query_mr": query_mr, "out_grad": out_grad, "norm_gain": norm_gain, "filter_se": filter_se, "filter_mr": filter_mr}


def causal_conv(padded, kernel, length):
    taps = kernel.shape[0]
    kern = kernel.astype(jnp.float32)

    def add_tap(index, total):
        tap = jnp.asarray(index).astype(jnp.int32)
        start = (jnp.int32(taps - 1) - tap).astype(jnp.int32)
        piece = lax.dynamic_slice_in_dim(padded, start, length, 0).astype(jnp.float32)
        weight_row = lax.dynamic_slice_in_dim(kern, tap, 1, 0)
        return total + piece * weight_row
    empty = jnp.zeros((length, padded.shape[1]), jnp.float32)
    return lax.fori_loop(0, taps, add_tap, empty)

def anti_conv(padded, kernel, length):
    taps = kernel.shape[0]
    kern = kernel.astype(jnp.float32)

    def add_tap(index, total):
        tap = jnp.asarray(index).astype(jnp.int32)
        piece = lax.dynamic_slice_in_dim(padded, tap, length, 0).astype(jnp.float32)
        weight_row = lax.dynamic_slice_in_dim(kern, tap, 1, 0)
        return total + piece * weight_row
    empty = jnp.zeros((length, padded.shape[1]), jnp.float32)
    return lax.fori_loop(0, taps, add_tap, empty)

def filter_grad(padded, grad_conv, taps, length):
    grad_f = grad_conv.astype(jnp.float32)

    def one_tap(carry, index):
        tap = index.astype(jnp.int32)
        start = (jnp.int32(taps - 1) - tap).astype(jnp.int32)
        piece = lax.dynamic_slice_in_dim(padded, start, length, 0).astype(jnp.float32)
        return (carry, lax.optimization_barrier(jnp.sum(grad_f * piece, axis=0)))
    tap_index = jnp.arange(taps).astype(jnp.int32)
    carry, rows = lax.scan(one_tap, jnp.zeros((), jnp.float32), tap_index)
    return rows

def reference(value_path, key_se, query_se, key_mr, query_mr, out_grad, norm_gain, filter_se, filter_mr):
    f32 = jnp.float32
    bf16 = jnp.bfloat16
    length = value_path.shape[0]
    prod_se = (key_se.astype(f32) * value_path.astype(f32)).astype(bf16)
    pad_se = jnp.pad(prod_se, ((SE_TAPS - 1, 0), (0, 0)))
    conv_se = causal_conv(pad_se, filter_se, length)
    mixed_se = query_se.astype(f32) * conv_se
    inv_rms = lax.rsqrt(lax.optimization_barrier(jnp.sum(mixed_se * mixed_se, axis=1, keepdims=True)) / D + 1e-06)
    gain = norm_gain.astype(f32)
    normed = (mixed_se * inv_rms * gain).astype(bf16)
    prod_mr = (key_mr.astype(f32) * normed.astype(f32)).astype(bf16)
    pad_mr = jnp.pad(prod_mr, ((MR_TAPS - 1, 0), (0, 0)))
    conv_mr = causal_conv(pad_mr, filter_mr, length)
    grad_query_mr = (out_grad.astype(f32) * conv_mr).astype(bf16)
    grad_conv_mr = (out_grad.astype(f32) * query_mr.astype(f32)).astype(bf16)
    grad_prod_mr = anti_conv(jnp.pad(grad_conv_mr, ((0, MR_TAPS - 1), (0, 0))), filter_mr, length)
    grad_key_mr = (grad_prod_mr * normed.astype(f32)).astype(bf16)
    grad_filter_mr = filter_grad(pad_mr, grad_conv_mr, MR_TAPS, length)
    grad_normed = grad_prod_mr * key_mr.astype(f32)
    scaled = grad_normed * gain
    grad_gain = lax.optimization_barrier(jnp.sum(grad_normed * mixed_se * inv_rms, axis=0))
    dot_sum = lax.optimization_barrier(jnp.sum(scaled * mixed_se, axis=1, keepdims=True))
    grad_mixed = inv_rms * scaled - mixed_se * (inv_rms * inv_rms * inv_rms) * dot_sum / D
    grad_query_se = (grad_mixed * conv_se).astype(bf16)
    grad_conv_se = (grad_mixed * query_se.astype(f32)).astype(bf16)
    grad_prod_se = anti_conv(jnp.pad(grad_conv_se, ((0, SE_TAPS - 1), (0, 0))), filter_se, length)
    grad_key_se = (grad_prod_se * value_path.astype(f32)).astype(bf16)
    grad_value = (grad_prod_se * key_se.astype(f32)).astype(bf16)
    grad_filter_se = filter_grad(pad_se, grad_conv_se, SE_TAPS, length)
    return (grad_value, grad_query_se, grad_key_se, grad_query_mr, grad_key_mr, grad_filter_se, grad_filter_mr, grad_gain)
```

```python
import jax
import jax.numpy as jnp
from jax import lax
from jax.sharding import PartitionSpec as P

D = 8192


def shifted(block, axis, distance):
    devices = range(lax.axis_size(axis))
    route = [(i - distance, i) for i in devices if i - distance in devices]
    return lax.ppermute(block, axis, route)


def depthwise(lhs, kernel):
    out = lax.conv_general_dilated(
        lhs[None],
        kernel[:, None, :],
        (1,),
        "VALID",
        dimension_numbers=("NWC", "WIO", "NWC"),
        feature_group_count=lhs.shape[1],
        preferred_element_type=jnp.float32,
    )
    return out[0]


def from_left(block, width):
    return shifted(block[block.shape[0] - width :], "ctx", 1)


def from_right(block, width):
    return shifted(block[:width], "ctx", -1)


def token_totals(parts):
    n = lax.axis_size("tp")
    spread = jnp.broadcast_to(parts[None], (n,) + parts.shape)
    return jnp.sum(lax.all_to_all(spread, "tp", 0, 0, tiled=True), axis=0)


def filter_totals(mr, small):
    bf16 = jnp.bfloat16
    n = lax.axis_size("ctx")
    taps, cols = mr.shape
    blocks = cols // 128
    groups = taps // 8
    tiles = mr.reshape(groups, 8, blocks, 128).transpose(0, 2, 1, 3).reshape(n, 8, 128)
    rows = small.reshape(8 * blocks, 1, 128)
    rows = jnp.pad(rows, ((0, n - 8 * blocks), (0, 0), (0, 0)))
    packed = jnp.concatenate([tiles, rows], axis=1).astype(bf16)
    packed = jnp.pad(packed, ((0, 0), (0, 7), (0, 0)))
    got = lax.all_to_all(packed, "ctx", 0, 0, tiled=True)
    total = lax.optimization_barrier(jnp.sum(got.astype(jnp.float32), axis=0)).astype(bf16)
    spread = jnp.broadcast_to(total[None], (n,) + total.shape)
    back = lax.all_to_all(spread, "ctx", 0, 0, tiled=True).astype(jnp.float32)
    mr_sum = back[:, :8].reshape(groups, blocks, 8, 128).transpose(0, 2, 1, 3).reshape(taps, cols)
    small_sum = back[: 8 * blocks, 8].reshape(8, cols)
    return mr_sum, small_sum


def shards(
    value_path, key_se, query_se, key_mr, query_mr, out_grad, norm_gain, filter_se, filter_mr
):
    f32 = jnp.float32
    bf16 = jnp.bfloat16
    se_taps = filter_se.shape[0]
    mr_taps = filter_mr.shape[0]
    prod_se = (key_se.astype(f32) * value_path.astype(f32)).astype(bf16)
    grad_conv_mr = (out_grad.astype(f32) * query_mr.astype(f32)).astype(bf16)
    rim_se = from_left(prod_se, se_taps - 1)
    rim_grad_mr = from_right(grad_conv_mr, mr_taps - 1)
    pad_se = jnp.concatenate([rim_se, prod_se], axis=0)
    pad_grad_mr = jnp.concatenate([grad_conv_mr, rim_grad_mr], axis=0)
    conv_se = depthwise(pad_se, filter_se[::-1])
    mixed_se = query_se.astype(f32) * conv_se
    grad_prod_mr = depthwise(pad_grad_mr, filter_mr)
    gain = norm_gain.astype(f32)
    grad_normed = grad_prod_mr * key_mr.astype(f32)
    scaled = grad_normed * gain
    square_part = jnp.sum(mixed_se * mixed_se, axis=1)
    dot_part = jnp.sum(scaled * mixed_se, axis=1)
    totals = token_totals(jnp.stack([square_part, dot_part]))
    inv_rms = lax.rsqrt(totals[0][:, None] / D + 1e-06)
    dot_sum = totals[1][:, None]
    normed = (mixed_se * inv_rms * gain).astype(bf16)
    prod_mr = (key_mr.astype(f32) * normed.astype(f32)).astype(bf16)
    grad_mixed = inv_rms * scaled - mixed_se * (inv_rms * inv_rms * inv_rms) * dot_sum / D
    grad_conv_se = (grad_mixed * query_se.astype(f32)).astype(bf16)
    rim_mr = from_left(prod_mr, mr_taps - 1)
    rim_grad_se = from_right(grad_conv_se, se_taps - 1)
    grad_key_mr = (grad_prod_mr * normed.astype(f32)).astype(bf16)
    grad_query_se = (grad_mixed * conv_se).astype(bf16)
    local_filter_mr = depthwise(pad_grad_mr, prod_mr)
    local_gain = jnp.sum(grad_normed * mixed_se * inv_rms, axis=0)
    local_filter_se = depthwise(pad_se, grad_conv_se)[::-1]
    grad_filter_mr, small = filter_totals(
        local_filter_mr, jnp.concatenate([local_filter_se, local_gain[None]], axis=0)
    )
    pad_mr = jnp.concatenate([rim_mr, prod_mr], axis=0)
    conv_mr = depthwise(pad_mr, filter_mr[::-1])
    grad_query_mr = (out_grad.astype(f32) * conv_mr).astype(bf16)
    grad_prod_se = depthwise(jnp.concatenate([grad_conv_se, rim_grad_se], axis=0), filter_se)
    grad_key_se = (grad_prod_se * value_path.astype(f32)).astype(bf16)
    grad_value = (grad_prod_se * key_se.astype(f32)).astype(bf16)
    return (
        grad_value,
        grad_query_se,
        grad_key_se,
        grad_query_mr,
        grad_key_mr,
        small[:se_taps],
        grad_filter_mr,
        small[se_taps],
    )


def solution(mesh):
    wide = P("ctx", "tp")
    return jax.shard_map(
        shards,
        mesh=mesh,
        in_specs=(wide,) * 6 + (P("tp"), P(None, "tp"), P(None, "tp")),
        out_specs=(wide,) * 5 + (P(None, "tp"), P(None, "tp"), P("tp")),
        check_vma=False,
    )
```

```python
import jax
import jax.numpy as jnp
import numpy as np
from jax import lax
from jax.experimental import pallas as pl
from jax.experimental.pallas import tpu as pltpu
from jax.sharding import PartitionSpec as P

D = 8192
WIDTH = 256
HALO = 16
F32 = jnp.float32
BF16 = jnp.bfloat16


def split(matrix):
    high = matrix.astype(jnp.bfloat16)
    low = (matrix - high.astype(np.float64)).astype(jnp.bfloat16)
    return high, low


def transforms():
    phase = 2 * np.pi * np.outer(np.arange(128) + 0.5, np.arange(256)) / 256
    forward = np.concatenate([np.cos(phase), -np.sin(phase)], axis=0)
    inverse = forward.T / 128
    f_high, f_low = split(forward)
    i_high, i_low = split(inverse)
    whole = np.concatenate([f_high, f_low], axis=1)
    half = np.concatenate([f_high[:, :128], f_low[:, :128]], axis=1)
    back = np.concatenate([i_high, i_high, i_low], axis=1)
    return jnp.asarray(whole), jnp.asarray(half), jnp.asarray(back[:128]), jnp.asarray(back[128:])


def to_spectrum(matrix, *rows):
    return jnp.dot(matrix, jnp.concatenate(rows + rows, axis=0), preferred_element_type=F32)


def from_spectrum(matrix, re, im):
    both = jnp.concatenate([re, im], axis=0)
    high = both.astype(BF16)
    low = (both - high.astype(F32)).astype(BF16)
    return jnp.dot(matrix, jnp.concatenate([high, low, high], axis=0), preferred_element_type=F32)


def correlated(matrix, kernel, signal):
    k_re, k_im = kernel[:128], kernel[128:]
    s_re, s_im = signal[:128], signal[128:]
    return from_spectrum(matrix, k_re * s_re + k_im * s_im, k_re * s_im - k_im * s_re)


def convolved(matrix, kernel, signal):
    k_re, k_im = kernel[:128], kernel[128:]
    s_re, s_im = signal[:128], signal[128:]
    return from_spectrum(matrix, k_re * s_re - k_im * s_im, k_re * s_im + k_im * s_re)


def lane_blocks(value):
    return sum(value[:, i : i + 128] for i in range(0, value.shape[1], 128))


def se_window(win, rim, key, value):
    prod = (key[...].astype(F32) * value[...].astype(F32)).astype(BF16)
    win[0:HALO] = rim[...].astype(F32)
    win[HALO:] = prod.astype(F32)


def se_kernel(key, value, query, rim, taps, conv, mixed, square, win):
    se_window(win, rim, key, value)
    f = taps[...].astype(F32)
    total = f[0:1] * win[HALO : HALO + 128]
    for j in range(1, f.shape[0]):
        total = total + f[j : j + 1] * win[HALO - j : HALO - j + 128]
    conv[...] = total
    m = query[...].astype(F32) * total
    mixed[...] = m

    @pl.when(pl.program_id(0) == 0)
    def _():
        square[...] = jnp.zeros_like(square)

    square[...] += lane_blocks(m * m)


def dot_kernel(
    grad, rim, taps, key, gain, mixed, square, whole, half, back, prod, spectrum, stats, acc
):
    kernel = to_spectrum(half[...], taps[...])
    signal = to_spectrum(whole[...], grad[...], rim[...])
    spectrum[...] = signal
    gp = correlated(back[...], kernel, signal)
    prod[...] = gp
    scaled = gp * key[...].astype(F32) * gain[...].astype(F32)

    @pl.when(pl.program_id(0) == 0)
    def _():
        acc[...] = jnp.zeros_like(acc)

    acc[...] += lane_blocks(scaled * mixed[...])

    @pl.when(pl.program_id(0) == pl.num_programs(0) - 1)
    def _():
        squares = jnp.sum(square[...].T, axis=0, keepdims=True)
        dots = jnp.sum(acc[...].T, axis=0, keepdims=True)
        row = lax.broadcasted_iota(jnp.int32, (8, 128), 0)
        both = jnp.where(row == 0, squares, jnp.where(row == 1, dots, 0.0))
        stats[...] = jnp.broadcast_to(both[None], stats.shape)


def main_kernel(
    stats, mixed, conv, prod, spectrum, key_mr, query_se, key_se, value, rim, gain, half, back,
    out_query_se, out_key_mr, out_prod_mr, out_conv_se, out_head, out_filter, out_small,
    win, inv_cols, dot_cols,
):
    @pl.when(pl.program_id(0) == 0)
    def _():
        sums = jnp.sum(stats[...], axis=0)
        inv = lax.rsqrt(sums[0:1] / D + 1e-06)
        dot = inv * inv * inv * sums[1:2] / D
        inv_cols[...] = jnp.broadcast_to(inv, (128, 128)).T
        dot_cols[...] = jnp.broadcast_to(dot, (128, 128)).T

    reps = mixed.shape[1] // 128
    inv = jnp.concatenate([inv_cols[...]] * reps, axis=1)
    dot = jnp.concatenate([dot_cols[...]] * reps, axis=1)
    m = mixed[...]
    gp = prod[...]
    g = gain[...].astype(F32)
    k = key_mr[...].astype(F32)
    scaled_mixed = m * inv
    normed = (scaled_mixed * g).astype(BF16).astype(F32)
    p = (k * normed).astype(BF16)
    out_prod_mr[...] = p
    out_key_mr[...] = (gp * normed).astype(BF16)
    grad = correlated(back[...], to_spectrum(half[...], p), spectrum[...])
    for b in range(reps):
        tile = grad[:, 128 * b : 128 * b + 128].reshape(out_filter.shape[0], 8, 128)
        out_filter[:, b] = tile.astype(BF16)
    grad_normed = gp * k
    gain_row = jnp.sum(grad_normed * scaled_mixed, axis=0, keepdims=True)
    grad_mixed = inv * (grad_normed * g) - m * dot
    out_query_se[...] = (grad_mixed * conv[...]).astype(BF16)
    gcs = (grad_mixed * query_se[...].astype(F32)).astype(BF16)
    out_conv_se[...] = gcs
    out_head[...] = gcs[:HALO]
    gcs = gcs.astype(F32)
    se_window(win, rim, key_se, value)
    taps = out_small.shape[0] - 1
    rows = [
        jnp.sum(gcs * win[HALO - j : HALO - j + 128], axis=0, keepdims=True) for j in range(taps)
    ]
    out_small[...] = jnp.concatenate(rows + [gain_row], axis=0)


def last_kernel(
    prod_mr, rim_mr, out_grad, taps_mr, conv_se, rim_se, taps_se, value, key_se, whole, half, back,
    out_query_mr, out_key_se, out_value, win,
):
    kernel = to_spectrum(half[...], taps_mr[...])
    signal = to_spectrum(whole[...], rim_mr[...], prod_mr[...])
    conv = convolved(back[...], kernel, signal)
    out_query_mr[...] = (out_grad[...].astype(F32) * conv).astype(BF16)
    win[0:128] = conv_se[...].astype(F32)
    win[128:] = rim_se[...].astype(F32)
    f = taps_se[...].astype(F32)
    total = f[0:1] * win[0:128]
    for j in range(1, f.shape[0]):
        total = total + f[j : j + 1] * win[j : j + 128]
    out_key_se[...] = (total * value[...].astype(F32)).astype(BF16)
    out_value[...] = (total * key_se[...].astype(F32)).astype(BF16)


def wide(rows):
    return pl.BlockSpec((rows, WIDTH), lambda i: (0, i))


def fixed(*shape):
    return pl.BlockSpec(shape, lambda i: (0,) * len(shape))


def call(kernel, cols, in_specs, out_specs, out_shape, scratch, flops, moved):
    return pl.pallas_call(
        kernel,
        grid=(cols // WIDTH,),
        in_specs=in_specs,
        out_specs=out_specs,
        out_shape=[jax.ShapeDtypeStruct(s, d) for s, d in out_shape],
        scratch_shapes=scratch,
        compiler_params=pltpu.CompilerParams(vmem_limit_bytes=40 * 1024 * 1024),
        cost_estimate=pl.CostEstimate(flops=flops, bytes_accessed=moved, transcendentals=0),
    )


def shifted(block, axis, distance):
    devices = range(lax.axis_size(axis))
    route = [(i - distance, i) for i in devices if i - distance in devices]
    return lax.ppermute(block, axis, route)


def filter_totals(tiles, small):
    n = lax.axis_size("ctx")
    cols = small.shape[1]
    rows = small.reshape(-1, 1, 1, 128).astype(BF16)
    rows = jnp.pad(rows, ((0, n - rows.shape[0]), (0, 0), (0, 1), (0, 0)))
    packed = jnp.concatenate([tiles.reshape(n, 4, 2, 128), rows], axis=1)
    got = lax.all_to_all(packed, "ctx", 0, 0, tiled=True)
    total = lax.optimization_barrier(jnp.sum(got.astype(F32), axis=0)).astype(BF16)
    spread = jnp.broadcast_to(total[None], (n,) + total.shape)
    back = lax.all_to_all(spread, "ctx", 0, 0, tiled=True)
    mr_sum = back[:, :4].reshape(tiles.shape).astype(F32).transpose(0, 2, 1, 3).reshape(-1, cols)
    small_sum = back[: cols // 16, 4, 0].astype(F32).reshape(8, cols)
    return mr_sum, small_sum


def shards(
    value_path, key_se, query_se, key_mr, query_mr, out_grad, norm_gain, filter_se, filter_mr
):
    tokens, cols = value_path.shape
    se_taps = filter_se.shape[0]
    full = (tokens, cols)
    whole, half, back_first, back_last = transforms()
    gain = norm_gain.reshape(1, cols)
    tail = (key_se[-HALO:].astype(F32) * value_path[-HALO:].astype(F32)).astype(BF16)
    grad_conv_mr = (out_grad.astype(F32) * query_mr.astype(F32)).astype(BF16)
    rim_se = shifted(tail, "ctx", 1)
    rim_grad_mr = shifted(grad_conv_mr, "ctx", -1)
    mats = [fixed(*whole.shape), fixed(*half.shape), fixed(*back_first.shape)]
    conv_se, mixed_se, square = call(
        se_kernel,
        cols,
        [wide(tokens)] * 3 + [wide(HALO), wide(se_taps)],
        [wide(tokens), wide(tokens), fixed(tokens, 128)],
        [(full, F32), (full, F32), ((tokens, 128), F32)],
        [pltpu.VMEM((tokens + HALO, WIDTH), F32)],
        18 * tokens * cols,
        14 * tokens * cols,
    )(key_se, value_path, query_se, rim_se, filter_se)
    grad_prod_mr, spectrum, stats = call(
        dot_kernel,
        cols,
        [wide(tokens)] * 4 + [wide(1), wide(tokens), fixed(tokens, 128)] + mats,
        [wide(tokens), wide(2 * tokens), fixed(8, 8, 128)],
        [(full, F32), ((2 * tokens, cols), F32), ((8, 8, 128), F32)],
        [pltpu.VMEM((tokens, 128), F32)],
        3000 * tokens * cols,
        24 * tokens * cols,
    )(grad_conv_mr, rim_grad_mr, filter_mr, key_mr, gain, mixed_se, square, whole, half, back_first)
    stats = lax.all_to_all(stats, "tp", 0, 0, tiled=True)
    groups = filter_mr.shape[0] // 8
    (
        grad_query_se, grad_key_mr, prod_mr, grad_conv_se, head, tiles, small
    ) = call(
        main_kernel,
        cols,
        [fixed(8, 8, 128)] + [wide(tokens)] * 3 + [wide(2 * tokens)] + [wide(tokens)] * 4
        + [wide(HALO), wide(1)] + mats[1:],
        [wide(tokens)] * 4
        + [wide(HALO), pl.BlockSpec((groups, WIDTH // 128, 8, 128), lambda i: (0, i, 0, 0))]
        + [wide(se_taps + 1)],
        [(full, BF16)] * 4
        + [((HALO, cols), BF16), ((groups, cols // 128, 8, 128), BF16), ((se_taps + 1, cols), F32)],
        [pltpu.VMEM((tokens + HALO, WIDTH), F32)] + [pltpu.VMEM((tokens, 128), F32)] * 2,
        2000 * tokens * cols,
        40 * tokens * cols,
    )(
        stats, mixed_se, conv_se, grad_prod_mr, spectrum, key_mr, query_se, key_se, value_path,
        rim_se, gain, half, back_first,
    )
    rim_mr = shifted(prod_mr, "ctx", 1)
    rim_grad_se = shifted(head, "ctx", -1)
    grad_filter_mr, small = filter_totals(tiles, small)
    grad_query_mr, grad_key_se, grad_value = call(
        last_kernel,
        cols,
        [wide(tokens)] * 5 + [wide(HALO), wide(se_taps)] + [wide(tokens)] * 2 + mats,
        [wide(tokens)] * 3,
        [(full, BF16)] * 3,
        [pltpu.VMEM((tokens + HALO, WIDTH), F32)],
        3000 * tokens * cols,
        20 * tokens * cols,
    )(
        prod_mr, rim_mr, out_grad, filter_mr, grad_conv_se, rim_grad_se, filter_se, value_path,
        key_se, whole, half, back_last,
    )
    return (
        grad_value,
        grad_query_se,
        grad_key_se,
        grad_query_mr,
        grad_key_mr,
        small[:se_taps],
        grad_filter_mr,
        small[se_taps],
    )


def solution(mesh):
    spread = P("ctx", "tp")
    return jax.shard_map(
        shards,
        mesh=mesh,
        in_specs=(spread,) * 6 + (P("tp"), P(None, "tp"), P(None, "tp")),
        out_specs=(spread,) * 5 + (P(None, "tp"), P(None, "tp"), P("tp")),
        check_vma=False,
    )
```

```python
import jax
import jax.numpy as jnp
import numpy as np
from jax import lax
from jax.experimental import pallas as pl
from jax.experimental.pallas import tpu as pltpu
from jax.sharding import PartitionSpec as P

D = 8192
WIDTH = 1024
HALO = 16
F32 = jnp.float32
BF16 = jnp.bfloat16


def split(matrix):
    high = matrix.astype(jnp.bfloat16)
    low = (matrix - high.astype(np.float64)).astype(jnp.bfloat16)
    return high, low


def transforms():
    phase = 2 * np.pi * np.outer(np.arange(128) + 0.5, np.arange(256)) / 256
    forward = np.concatenate([np.cos(phase), -np.sin(phase)], axis=0)
    inverse = forward.T / 128
    f_high, f_low = split(forward)
    i_high, i_low = split(inverse)
    whole = np.concatenate([f_high, f_low], axis=1)
    half = np.concatenate([f_high[:, :128], f_low[:, :128]], axis=1)
    later = np.concatenate([f_high[:, 128:], f_low[:, 128:]], axis=1)
    back = np.concatenate([i_high, i_high, i_low], axis=1)
    return [jnp.asarray(m) for m in (whole, half, later, back[:128], back[128:])]


def to_spectrum(matrix, *rows):
    return jnp.dot(matrix, jnp.concatenate(rows + rows, axis=0), preferred_element_type=F32)


def from_spectrum(matrix, re, im):
    both = jnp.concatenate([re, im], axis=0)
    high = both.astype(BF16)
    low = (both - high.astype(F32)).astype(BF16)
    return jnp.dot(matrix, jnp.concatenate([high, low, high], axis=0), preferred_element_type=F32)


def correlated(matrix, kernel, signal):
    k_re, k_im = kernel[:128], kernel[128:]
    s_re, s_im = signal[:128], signal[128:]
    return from_spectrum(matrix, k_re * s_re + k_im * s_im, k_re * s_im - k_im * s_re)


def convolved(matrix, kernel, signal):
    k_re, k_im = kernel[:128], kernel[128:]
    s_re, s_im = signal[:128], signal[128:]
    return from_spectrum(matrix, k_re * s_re - k_im * s_im, k_re * s_im + k_im * s_re)


def lane_blocks(value):
    return sum(value[:, i : i + 128] for i in range(0, value.shape[1], 128))


def se_window(win, rim, key, value):
    prod = (key[...].astype(F32) * value[...].astype(F32)).astype(BF16)
    win[0:HALO] = rim[...].astype(F32)
    win[HALO:] = prod.astype(F32)


def se_kernel(
    key, value, query, rim, taps, grad, taps_mr, half, conv, mixed, square, kernel, near, win
):
    kernel[...] = to_spectrum(half[...], taps_mr[...])
    near[...] = to_spectrum(half[...], grad[...])
    se_window(win, rim, key, value)
    f = taps[...].astype(F32)
    total = f[0:1] * win[HALO : HALO + 128]
    for j in range(1, f.shape[0]):
        total = total + f[j : j + 1] * win[HALO - j : HALO - j + 128]
    conv[...] = total
    m = query[...].astype(F32) * total
    mixed[...] = m

    @pl.when(pl.program_id(0) == 0)
    def _():
        square[...] = jnp.zeros_like(square)

    square[...] += lane_blocks(m * m)


def dot_kernel(
    near, rim, kernel, key, gain, mixed, square, later, back, prod, spectrum, stats, acc
):
    signal = near[...] + to_spectrum(later[...], rim[...])
    spectrum[...] = signal
    gp = correlated(back[...], kernel[...], signal)
    prod[...] = gp
    scaled = gp * key[...].astype(F32) * gain[...].astype(F32)

    @pl.when(pl.program_id(0) == 0)
    def _():
        acc[...] = jnp.zeros_like(acc)

    acc[...] += lane_blocks(scaled * mixed[...])

    @pl.when(pl.program_id(0) == pl.num_programs(0) - 1)
    def _():
        squares = jnp.sum(square[...].T, axis=0, keepdims=True)
        dots = jnp.sum(acc[...].T, axis=0, keepdims=True)
        row = lax.broadcasted_iota(jnp.int32, (8, 128), 0)
        both = jnp.where(row == 0, squares, jnp.where(row == 1, dots, 0.0))
        stats[...] = jnp.broadcast_to(both[None], stats.shape)


def main_kernel(
    stats, mixed, conv, prod, spectrum, key_mr, query_se, key_se, value, rim, gain, half, back,
    out_query_se, out_key_mr, out_prod_mr, out_conv_se, out_head, out_filter, out_small,
    win, inv_cols, dot_cols,
):
    @pl.when(pl.program_id(0) == 0)
    def _():
        sums = jnp.sum(stats[...], axis=0)
        inv = lax.rsqrt(sums[0:1] / D + 1e-06)
        dot = inv * inv * inv * sums[1:2] / D
        inv_cols[...] = jnp.broadcast_to(inv, (128, 128)).T
        dot_cols[...] = jnp.broadcast_to(dot, (128, 128)).T

    reps = mixed.shape[1] // 128
    inv = jnp.concatenate([inv_cols[...]] * reps, axis=1)
    dot = jnp.concatenate([dot_cols[...]] * reps, axis=1)
    m = mixed[...]
    gp = prod[...]
    g = gain[...].astype(F32)
    k = key_mr[...].astype(F32)
    scaled_mixed = m * inv
    normed = (scaled_mixed * g).astype(BF16).astype(F32)
    p = (k * normed).astype(BF16)
    out_prod_mr[...] = p
    out_key_mr[...] = (gp * normed).astype(BF16)
    grad = correlated(back[...], to_spectrum(half[...], p), spectrum[...])
    for b in range(reps):
        tile = grad[:, 128 * b : 128 * b + 128].reshape(out_filter.shape[0], 8, 128)
        out_filter[:, b] = tile.astype(BF16)
    grad_normed = gp * k
    gain_row = jnp.sum(grad_normed * scaled_mixed, axis=0, keepdims=True)
    grad_mixed = inv * (grad_normed * g) - m * dot
    out_query_se[...] = (grad_mixed * conv[...]).astype(BF16)
    gcs = (grad_mixed * query_se[...].astype(F32)).astype(BF16)
    out_conv_se[...] = gcs
    out_head[...] = gcs[:HALO]
    gcs = gcs.astype(F32)
    se_window(win, rim, key_se, value)
    taps = out_small.shape[0] - 1
    rows = [
        jnp.sum(gcs * win[HALO - j : HALO - j + 128], axis=0, keepdims=True) for j in range(taps)
    ]
    out_small[...] = jnp.concatenate(rows + [gain_row], axis=0)


def last_kernel(
    prod_mr, rim_mr, out_grad, kernel, conv_se, rim_se, taps_se, value, key_se, whole, back,
    out_query_mr, out_key_se, out_value, win,
):
    signal = to_spectrum(whole[...], rim_mr[...], prod_mr[...])
    conv = convolved(back[...], kernel[...], signal)
    out_query_mr[...] = (out_grad[...].astype(F32) * conv).astype(BF16)
    win[0:128] = conv_se[...].astype(F32)
    win[128:] = rim_se[...].astype(F32)
    f = taps_se[...].astype(F32)
    total = f[0:1] * win[0:128]
    for j in range(1, f.shape[0]):
        total = total + f[j : j + 1] * win[j : j + 128]
    out_key_se[...] = (total * value[...].astype(F32)).astype(BF16)
    out_value[...] = (total * key_se[...].astype(F32)).astype(BF16)


def gate_kernel(got, rim_mr, rim_se, out):
    del got, rim_mr, rim_se, out


def wide(rows):
    return pl.BlockSpec((rows, WIDTH), lambda i: (0, i))


def fixed(*shape):
    return pl.BlockSpec(shape, lambda i: (0,) * len(shape))


def call(kernel, cols, in_specs, out_specs, out_shape, scratch, flops, moved):
    return pl.pallas_call(
        kernel,
        grid=(cols // WIDTH,),
        in_specs=in_specs,
        out_specs=out_specs,
        out_shape=[jax.ShapeDtypeStruct(s, d) for s, d in out_shape],
        scratch_shapes=scratch,
        compiler_params=pltpu.CompilerParams(vmem_limit_bytes=40 * 1024 * 1024),
        cost_estimate=pl.CostEstimate(flops=flops, bytes_accessed=moved, transcendentals=0),
    )


def shifted(block, axis, distance):
    devices = range(lax.axis_size(axis))
    route = [(i - distance, i) for i in devices if i - distance in devices]
    return lax.ppermute(block, axis, route)


def filter_totals(tiles, small, rims):
    n = lax.axis_size("ctx")
    cols = small.shape[1]
    rows = small.reshape(8, -1, 128).transpose(1, 0, 2).reshape(-1, 1, 1, 128).astype(BF16)
    rows = jnp.pad(rows, ((0, n - rows.shape[0]), (0, 0), (0, 1), (0, 0)))
    packed = jnp.concatenate([tiles.reshape(n, 4, 2, 128), rows], axis=1)
    got = lax.all_to_all(packed, "ctx", 0, 0, tiled=True)
    anywhere = pl.BlockSpec(memory_space=pl.ANY)
    got = pl.pallas_call(
        gate_kernel,
        in_specs=[anywhere] * 3,
        out_specs=anywhere,
        out_shape=jax.ShapeDtypeStruct(got.shape, BF16),
        input_output_aliases={0: 0},
    )(got, *rims)
    total = lax.optimization_barrier(jnp.sum(got.astype(F32), axis=0)).astype(BF16)
    spread = jnp.broadcast_to(total[None], (n,) + total.shape)
    back = lax.all_to_all(spread, "ctx", 0, 0, tiled=True)
    mr_sum = back[:, :4].reshape(tiles.shape).astype(F32).transpose(0, 2, 1, 3).reshape(-1, cols)
    small_sum = back[: cols // 16, 4, 0].astype(F32).reshape(-1, 8, 128)
    return mr_sum, small_sum.transpose(1, 0, 2).reshape(8, cols)


def shards(
    value_path, key_se, query_se, key_mr, query_mr, out_grad, norm_gain, filter_se, filter_mr
):
    tokens, cols = value_path.shape
    se_taps = filter_se.shape[0]
    full = (tokens, cols)
    whole, half, later, back_first, back_last = transforms()
    gain = norm_gain.reshape(1, cols)
    tail = (key_se[-HALO:].astype(F32) * value_path[-HALO:].astype(F32)).astype(BF16)
    grad_conv_mr = (out_grad.astype(F32) * query_mr.astype(F32)).astype(BF16)
    rim_se = shifted(tail, "ctx", 1)
    rim_grad_mr = shifted(grad_conv_mr, "ctx", -1)
    half_spec, back_spec = fixed(*half.shape), fixed(*back_first.shape)
    spectral = (2 * tokens, cols)
    conv_se, mixed_se, square, kernel_mr, near = call(
        se_kernel,
        cols,
        [wide(tokens)] * 3 + [wide(HALO), wide(se_taps)] + [wide(tokens)] * 2 + [half_spec],
        [wide(tokens), wide(tokens), fixed(tokens, 128)] + [wide(2 * tokens)] * 2,
        [(full, F32), (full, F32), ((tokens, 128), F32), (spectral, F32), (spectral, F32)],
        [pltpu.VMEM((tokens + HALO, WIDTH), F32)],
        2000 * tokens * cols,
        14 * tokens * cols,
    )(key_se, value_path, query_se, rim_se, filter_se, grad_conv_mr, filter_mr, half)
    grad_prod_mr, spectrum, stats = call(
        dot_kernel,
        cols,
        [wide(2 * tokens), wide(tokens), wide(2 * tokens), wide(tokens), wide(1), wide(tokens)]
        + [fixed(tokens, 128), half_spec, back_spec],
        [wide(tokens), wide(2 * tokens), fixed(8, 8, 128)],
        [(full, F32), (spectral, F32), ((8, 8, 128), F32)],
        [pltpu.VMEM((tokens, 128), F32)],
        3000 * tokens * cols,
        24 * tokens * cols,
    )(near, rim_grad_mr, kernel_mr, key_mr, gain, mixed_se, square, later, back_first)
    stats = lax.all_to_all(stats, "tp", 0, 0, tiled=True)
    groups = filter_mr.shape[0] // 8
    (
        grad_query_se, grad_key_mr, prod_mr, grad_conv_se, head, tiles, small
    ) = call(
        main_kernel,
        cols,
        [fixed(8, 8, 128)] + [wide(tokens)] * 3 + [wide(2 * tokens)] + [wide(tokens)] * 4
        + [wide(HALO), wide(1), half_spec, back_spec],
        [wide(tokens)] * 4
        + [wide(HALO), pl.BlockSpec((groups, WIDTH // 128, 8, 128), lambda i: (0, i, 0, 0))]
        + [wide(se_taps + 1)],
        [(full, BF16)] * 4
        + [((HALO, cols), BF16), ((groups, cols // 128, 8, 128), BF16), ((se_taps + 1, cols), F32)],
        [pltpu.VMEM((tokens + HALO, WIDTH), F32)] + [pltpu.VMEM((tokens, 128), F32)] * 2,
        2000 * tokens * cols,
        40 * tokens * cols,
    )(
        stats, mixed_se, conv_se, grad_prod_mr, spectrum, key_mr, query_se, key_se, value_path,
        rim_se, gain, half, back_first,
    )
    rim_mr = shifted(prod_mr, "ctx", 1)
    rim_grad_se = shifted(head, "ctx", -1)
    grad_filter_mr, small = filter_totals(tiles, small, (rim_mr, rim_grad_se))
    grad_query_mr, grad_key_se, grad_value = call(
        last_kernel,
        cols,
        [wide(tokens)] * 3 + [wide(2 * tokens), wide(tokens), wide(HALO), wide(se_taps)]
        + [wide(tokens)] * 2 + [fixed(*whole.shape), back_spec],
        [wide(tokens)] * 3,
        [(full, BF16)] * 3,
        [pltpu.VMEM((tokens + HALO, WIDTH), F32)],
        3000 * tokens * cols,
        20 * tokens * cols,
    )(
        prod_mr, rim_mr, out_grad, kernel_mr, grad_conv_se, rim_grad_se, filter_se, value_path,
        key_se, whole, back_last,
    )
    return (
        grad_value,
        grad_query_se,
        grad_key_se,
        grad_query_mr,
        grad_key_mr,
        small[:se_taps],
        grad_filter_mr,
        small[se_taps],
    )


def solution(mesh):
    spread = P("ctx", "tp")
    return jax.shard_map(
        shards,
        mesh=mesh,
        in_specs=(spread,) * 6 + (P("tp"), P(None, "tp"), P(None, "tp")),
        out_specs=(spread,) * 5 + (P(None, "tp"), P(None, "tp"), P("tp")),
        check_vma=False,
    )
```

```python
import jax
import jax.numpy as jnp
import numpy as np
from jax import lax
from jax.experimental import pallas as pl
from jax.experimental.pallas import tpu as pltpu
from jax.sharding import PartitionSpec as P

D = 8192
WIDTH = 1024
HALO = 16
F32 = jnp.float32
BF16 = jnp.bfloat16


def split(matrix):
    high = matrix.astype(jnp.bfloat16)
    low = (matrix - high.astype(np.float64)).astype(jnp.bfloat16)
    return high, low


def transforms():
    phase = 2 * np.pi * np.outer(np.arange(128) + 0.5, np.arange(256)) / 256
    forward = np.concatenate([np.cos(phase), -np.sin(phase)], axis=0)
    inverse = forward.T / 128
    f_high, f_low = split(forward)
    i_high, i_low = split(inverse)
    whole = np.concatenate([f_high, f_low], axis=1)
    half = np.concatenate([f_high[:, :128], f_low[:, :128]], axis=1)
    later = np.concatenate([f_high[:, 128:], f_low[:, 128:]], axis=1)
    back = np.concatenate([i_high, i_high, i_low], axis=1)
    return [jnp.asarray(m) for m in (whole, half, later, back[:128], back[128:])]


def to_spectrum(matrix, *rows):
    return jnp.dot(matrix, jnp.concatenate(rows + rows, axis=0), preferred_element_type=F32)


def from_spectrum(matrix, re, im):
    both = jnp.concatenate([re, im], axis=0)
    high = both.astype(BF16)
    low = (both - high.astype(F32)).astype(BF16)
    return jnp.dot(matrix, jnp.concatenate([high, low, high], axis=0), preferred_element_type=F32)


def correlated(matrix, kernel, signal):
    k_re, k_im = kernel[:128], kernel[128:]
    s_re, s_im = signal[:128], signal[128:]
    return from_spectrum(matrix, k_re * s_re + k_im * s_im, k_re * s_im - k_im * s_re)


def convolved(matrix, kernel, signal):
    k_re, k_im = kernel[:128], kernel[128:]
    s_re, s_im = signal[:128], signal[128:]
    return from_spectrum(matrix, k_re * s_re - k_im * s_im, k_re * s_im + k_im * s_re)


def lane_blocks(value):
    return sum(value[:, i : i + 128] for i in range(0, value.shape[1], 128))


def se_window(win, rim, key, value):
    prod = (key[...].astype(F32) * value[...].astype(F32)).astype(BF16)
    win[0:HALO] = rim[...].astype(F32)
    win[HALO:] = prod.astype(F32)


def spectra_kernel(grad, taps, half, kernel, near):
    kernel[...] = to_spectrum(half[...], taps[...])
    near[...] = to_spectrum(half[...], grad[...])


def se_kernel(key, value, query, rim, taps, conv, mixed, square, win):
    se_window(win, rim, key, value)
    f = taps[...].astype(F32)
    total = f[0:1] * win[HALO : HALO + 128]
    for j in range(1, f.shape[0]):
        total = total + f[j : j + 1] * win[HALO - j : HALO - j + 128]
    conv[...] = total
    m = query[...].astype(F32) * total
    mixed[...] = m

    @pl.when(pl.program_id(0) == 0)
    def _():
        square[...] = jnp.zeros_like(square)

    square[...] += lane_blocks(m * m)


def dot_kernel(
    near, rim, kernel, key, gain, mixed, square, later, back, prod, spectrum, stats, acc
):
    signal = near[...] + to_spectrum(later[...], rim[...])
    spectrum[...] = signal
    gp = correlated(back[...], kernel[...], signal)
    prod[...] = gp
    scaled = gp * key[...].astype(F32) * gain[...].astype(F32)

    @pl.when(pl.program_id(0) == 0)
    def _():
        acc[...] = jnp.zeros_like(acc)

    acc[...] += lane_blocks(scaled * mixed[...])

    @pl.when(pl.program_id(0) == pl.num_programs(0) - 1)
    def _():
        squares = jnp.sum(square[...].T, axis=0, keepdims=True)
        dots = jnp.sum(acc[...].T, axis=0, keepdims=True)
        row = lax.broadcasted_iota(jnp.int32, (8, 128), 0)
        both = jnp.where(row == 0, squares, jnp.where(row == 1, dots, 0.0))
        stats[...] = jnp.broadcast_to(both[None], stats.shape)


def main_kernel(
    stats, mixed, conv, prod, spectrum, key_mr, query_se, key_se, value, rim, gain, half, back,
    out_query_se, out_key_mr, out_prod_mr, out_conv_se, out_head, out_filter, out_small,
    win, inv_cols, dot_cols,
):
    @pl.when(pl.program_id(0) == 0)
    def _():
        sums = jnp.sum(stats[...], axis=0)
        inv = lax.rsqrt(sums[0:1] / D + 1e-06)
        dot = inv * inv * inv * sums[1:2] / D
        inv_cols[...] = jnp.broadcast_to(inv, (128, 128)).T
        dot_cols[...] = jnp.broadcast_to(dot, (128, 128)).T

    reps = mixed.shape[1] // 128
    inv = jnp.concatenate([inv_cols[...]] * reps, axis=1)
    dot = jnp.concatenate([dot_cols[...]] * reps, axis=1)
    m = mixed[...]
    gp = prod[...]
    g = gain[...].astype(F32)
    k = key_mr[...].astype(F32)
    scaled_mixed = m * inv
    normed = (scaled_mixed * g).astype(BF16).astype(F32)
    p = (k * normed).astype(BF16)
    out_prod_mr[...] = p
    out_key_mr[...] = (gp * normed).astype(BF16)
    grad = correlated(back[...], to_spectrum(half[...], p), spectrum[...])
    for b in range(reps):
        tile = grad[:, 128 * b : 128 * b + 128].reshape(out_filter.shape[0], 8, 128)
        out_filter[:, b] = tile.astype(BF16)
    grad_normed = gp * k
    gain_row = jnp.sum(grad_normed * scaled_mixed, axis=0, keepdims=True)
    grad_mixed = inv * (grad_normed * g) - m * dot
    out_query_se[...] = (grad_mixed * conv[...]).astype(BF16)
    gcs = (grad_mixed * query_se[...].astype(F32)).astype(BF16)
    out_conv_se[...] = gcs
    out_head[...] = gcs[:HALO]
    gcs = gcs.astype(F32)
    se_window(win, rim, key_se, value)
    taps = out_small.shape[0] - 1
    rows = [
        jnp.sum(gcs * win[HALO - j : HALO - j + 128], axis=0, keepdims=True) for j in range(taps)
    ]
    out_small[...] = jnp.concatenate(rows + [gain_row], axis=0)


def last_kernel(
    prod_mr, rim_mr, out_grad, kernel, conv_se, rim_se, taps_se, value, key_se, whole, back,
    out_query_mr, out_key_se, out_value, win,
):
    signal = to_spectrum(whole[...], rim_mr[...], prod_mr[...])
    conv = convolved(back[...], kernel[...], signal)
    out_query_mr[...] = (out_grad[...].astype(F32) * conv).astype(BF16)
    win[0:128] = conv_se[...].astype(F32)
    win[128:] = rim_se[...].astype(F32)
    f = taps_se[...].astype(F32)
    total = f[0:1] * win[0:128]
    for j in range(1, f.shape[0]):
        total = total + f[j : j + 1] * win[j : j + 128]
    out_key_se[...] = (total * value[...].astype(F32)).astype(BF16)
    out_value[...] = (total * key_se[...].astype(F32)).astype(BF16)


def gate_kernel(total, rim_mr, rim_se, out):
    del total, rim_mr, rim_se, out


def wide(rows):
    return pl.BlockSpec((rows, WIDTH), lambda i: (0, i))


def fixed(*shape):
    return pl.BlockSpec(shape, lambda i: (0,) * len(shape))


def call(kernel, cols, in_specs, out_specs, out_shape, scratch, flops, moved):
    return pl.pallas_call(
        kernel,
        grid=(cols // WIDTH,),
        in_specs=in_specs,
        out_specs=out_specs,
        out_shape=[jax.ShapeDtypeStruct(s, d) for s, d in out_shape],
        scratch_shapes=scratch,
        compiler_params=pltpu.CompilerParams(vmem_limit_bytes=40 * 1024 * 1024),
        cost_estimate=pl.CostEstimate(flops=flops, bytes_accessed=moved, transcendentals=0),
    )


def shifted(block, axis, distance):
    devices = range(lax.axis_size(axis))
    route = [(i - distance, i) for i in devices if i - distance in devices]
    return lax.ppermute(block, axis, route)


def filter_totals(tiles, small, rims):
    n = lax.axis_size("ctx")
    plane = n // 2
    planes = [list(range(plane)), list(range(plane, n))]
    cols = small.shape[1]
    rows = small.reshape(8, -1, 128).transpose(1, 0, 2).reshape(plane, 1, 1, 128).astype(BF16)
    rows = jnp.pad(rows, ((0, 0), (0, 0), (0, 1), (0, 0)))
    packed = jnp.concatenate([tiles.reshape(plane, 8, 2, 128), rows], axis=1)
    got = lax.all_to_all(packed, "ctx", 0, 0, axis_index_groups=planes, tiled=True)
    part = jnp.sum(got.astype(F32), axis=0)
    total = part + lax.ppermute(part, "ctx", [(i, (i + plane) % n) for i in range(n)])
    anywhere = pl.BlockSpec(memory_space=pl.ANY)
    total = pl.pallas_call(
        gate_kernel,
        in_specs=[anywhere] * 3,
        out_specs=anywhere,
        out_shape=jax.ShapeDtypeStruct(total.shape, F32),
        input_output_aliases={0: 0},
    )(total, *rims)
    spread = jnp.broadcast_to(total.astype(BF16)[None], (plane,) + total.shape)
    back = lax.all_to_all(spread, "ctx", 0, 0, axis_index_groups=planes, tiled=True)
    mr_sum = back[:, :8].reshape(tiles.shape).astype(F32).transpose(0, 2, 1, 3).reshape(-1, cols)
    small_sum = back[:, 8, 0].astype(F32).reshape(-1, 8, 128)
    return mr_sum, small_sum.transpose(1, 0, 2).reshape(8, cols)


def shards(
    value_path, key_se, query_se, key_mr, query_mr, out_grad, norm_gain, filter_se, filter_mr
):
    tokens, cols = value_path.shape
    se_taps = filter_se.shape[0]
    full = (tokens, cols)
    whole, half, later, back_first, back_last = transforms()
    gain = norm_gain.reshape(1, cols)
    tail = (key_se[-HALO:].astype(F32) * value_path[-HALO:].astype(F32)).astype(BF16)
    grad_conv_mr = (out_grad.astype(F32) * query_mr.astype(F32)).astype(BF16)
    rim_se = shifted(tail, "ctx", 1)
    rim_grad_mr = shifted(grad_conv_mr, "ctx", -1)
    half_spec, back_spec = fixed(*half.shape), fixed(*back_first.shape)
    spectral = (2 * tokens, cols)
    kernel_mr, near = call(
        spectra_kernel,
        cols,
        [wide(tokens)] * 2 + [half_spec],
        [wide(2 * tokens)] * 2,
        [(spectral, F32)] * 2,
        [],
        2000 * tokens * cols,
        20 * tokens * cols,
    )(grad_conv_mr, filter_mr, half)
    conv_se, mixed_se, square = call(
        se_kernel,
        cols,
        [wide(tokens)] * 3 + [wide(HALO), wide(se_taps)],
        [wide(tokens), wide(tokens), fixed(tokens, 128)],
        [(full, F32), (full, F32), ((tokens, 128), F32)],
        [pltpu.VMEM((tokens + HALO, WIDTH), F32)],
        18 * tokens * cols,
        14 * tokens * cols,
    )(key_se, value_path, query_se, rim_se, filter_se)
    grad_prod_mr, spectrum, stats = call(
        dot_kernel,
        cols,
        [wide(2 * tokens), wide(tokens), wide(2 * tokens), wide(tokens), wide(1), wide(tokens)]
        + [fixed(tokens, 128), half_spec, back_spec],
        [wide(tokens), wide(2 * tokens), fixed(8, 8, 128)],
        [(full, F32), (spectral, F32), ((8, 8, 128), F32)],
        [pltpu.VMEM((tokens, 128), F32)],
        3000 * tokens * cols,
        24 * tokens * cols,
    )(near, rim_grad_mr, kernel_mr, key_mr, gain, mixed_se, square, later, back_first)
    stats = lax.all_to_all(stats, "tp", 0, 0, tiled=True)
    groups = filter_mr.shape[0] // 8
    (
        grad_query_se, grad_key_mr, prod_mr, grad_conv_se, head, tiles, small
    ) = call(
        main_kernel,
        cols,
        [fixed(8, 8, 128)] + [wide(tokens)] * 3 + [wide(2 * tokens)] + [wide(tokens)] * 4
        + [wide(HALO), wide(1), half_spec, back_spec],
        [wide(tokens)] * 4
        + [wide(HALO), pl.BlockSpec((groups, WIDTH // 128, 8, 128), lambda i: (0, i, 0, 0))]
        + [wide(se_taps + 1)],
        [(full, BF16)] * 4
        + [((HALO, cols), BF16), ((groups, cols // 128, 8, 128), BF16), ((se_taps + 1, cols), F32)],
        [pltpu.VMEM((tokens + HALO, WIDTH), F32)] + [pltpu.VMEM((tokens, 128), F32)] * 2,
        2000 * tokens * cols,
        40 * tokens * cols,
    )(
        stats, mixed_se, conv_se, grad_prod_mr, spectrum, key_mr, query_se, key_se, value_path,
        rim_se, gain, half, back_first,
    )
    rim_mr = shifted(prod_mr, "ctx", 1)
    rim_grad_se = shifted(head, "ctx", -1)
    grad_filter_mr, small = filter_totals(tiles, small, (rim_mr, rim_grad_se))
    grad_query_mr, grad_key_se, grad_value = call(
        last_kernel,
        cols,
        [wide(tokens)] * 3 + [wide(2 * tokens), wide(tokens), wide(HALO), wide(se_taps)]
        + [wide(tokens)] * 2 + [fixed(*whole.shape), back_spec],
        [wide(tokens)] * 3,
        [(full, BF16)] * 3,
        [pltpu.VMEM((tokens + HALO, WIDTH), F32)],
        3000 * tokens * cols,
        20 * tokens * cols,
    )(
        prod_mr, rim_mr, out_grad, kernel_mr, grad_conv_se, rim_grad_se, filter_se, value_path,
        key_se, whole, back_last,
    )
    return (
        grad_value,
        grad_query_se,
        grad_key_se,
        grad_query_mr,
        grad_key_mr,
        small[:se_taps],
        grad_filter_mr,
        small[se_taps],
    )


def solution(mesh):
    spread = P("ctx", "tp")
    return jax.shard_map(
        shards,
        mesh=mesh,
        in_specs=(spread,) * 6 + (P("tp"), P(None, "tp"), P(None, "tp")),
        out_specs=(spread,) * 5 + (P(None, "tp"), P(None, "tp"), P("tp")),
        check_vma=False,
    )
```

```python
import jax
import jax.numpy as jnp
import numpy as np
from jax import lax
from jax.experimental import pallas as pl
from jax.experimental.pallas import tpu as pltpu
from jax.sharding import PartitionSpec as P

D = 8192
WIDTH = 1024
HALO = 16
F32 = jnp.float32
BF16 = jnp.bfloat16


def split(matrix):
    high = matrix.astype(jnp.bfloat16)
    low = (matrix - high.astype(np.float64)).astype(jnp.bfloat16)
    return high, low


def transforms():
    phase = 2 * np.pi * np.outer(np.arange(128) + 0.5, np.arange(256)) / 256
    forward = np.concatenate([np.cos(phase), -np.sin(phase)], axis=0)
    inverse = forward.T / 128
    f_high, f_low = split(forward)
    i_high, i_low = split(inverse)
    whole = np.concatenate([f_high, f_low], axis=1)
    half = np.concatenate([f_high[:, :128], f_low[:, :128]], axis=1)
    later = np.concatenate([f_high[:, 128:], f_low[:, 128:]], axis=1)
    back = np.concatenate([i_high, i_high, i_low], axis=1)
    return [jnp.asarray(m) for m in (whole, half, later, back[:128], back[128:])]


def to_spectrum(matrix, *rows):
    return jnp.dot(matrix, jnp.concatenate(rows + rows, axis=0), preferred_element_type=F32)


def from_spectrum(matrix, re, im):
    both = jnp.concatenate([re, im], axis=0)
    high = both.astype(BF16)
    low = (both - high.astype(F32)).astype(BF16)
    return jnp.dot(matrix, jnp.concatenate([high, low, high], axis=0), preferred_element_type=F32)


def correlated(matrix, kernel, signal):
    k_re, k_im = kernel[:128], kernel[128:]
    s_re, s_im = signal[:128], signal[128:]
    return from_spectrum(matrix, k_re * s_re + k_im * s_im, k_re * s_im - k_im * s_re)


def convolved(matrix, kernel, signal):
    k_re, k_im = kernel[:128], kernel[128:]
    s_re, s_im = signal[:128], signal[128:]
    return from_spectrum(matrix, k_re * s_re - k_im * s_im, k_re * s_im + k_im * s_re)


def lane_blocks(value):
    return sum(value[:, i : i + 128] for i in range(0, value.shape[1], 128))


def se_window(win, rim, key, value):
    prod = (key[...].astype(F32) * value[...].astype(F32)).astype(BF16)
    win[0:HALO] = rim[...].astype(F32)
    win[HALO:] = prod.astype(F32)


def spectra_kernel(grad, taps, half, kernel, near):
    kernel[...] = to_spectrum(half[...], taps[...])
    near[...] = to_spectrum(half[...], grad[...])


def se_kernel(key, value, query, rim, taps, conv, mixed, square, win):
    se_window(win, rim, key, value)
    f = taps[...].astype(F32)
    total = f[0:1] * win[HALO : HALO + 128]
    for j in range(1, f.shape[0]):
        total = total + f[j : j + 1] * win[HALO - j : HALO - j + 128]
    conv[...] = total
    m = query[...].astype(F32) * total
    mixed[...] = m

    @pl.when(pl.program_id(0) == 0)
    def _():
        square[...] = jnp.zeros_like(square)

    square[...] += lane_blocks(m * m)


def dot_kernel(
    near, rim, kernel, key, gain, mixed, square, later, back, prod, spectrum, stats, acc
):
    signal = near[...] + to_spectrum(later[...], rim[...])
    spectrum[...] = signal
    gp = correlated(back[...], kernel[...], signal)
    prod[...] = gp
    scaled = gp * key[...].astype(F32) * gain[...].astype(F32)

    @pl.when(pl.program_id(0) == 0)
    def _():
        acc[...] = jnp.zeros_like(acc)

    acc[...] += lane_blocks(scaled * mixed[...])

    @pl.when(pl.program_id(0) == pl.num_programs(0) - 1)
    def _():
        squares = jnp.sum(square[...].T, axis=0, keepdims=True)
        dots = jnp.sum(acc[...].T, axis=0, keepdims=True)
        row = lax.broadcasted_iota(jnp.int32, (8, 128), 0)
        both = jnp.where(row == 0, squares, jnp.where(row == 1, dots, 0.0))
        stats[...] = jnp.broadcast_to(both[None], stats.shape)


def main_kernel(
    stats, mixed, conv, prod, spectrum, key_mr, query_se, key_se, value, rim, gain, half, back,
    out_query_se, out_key_mr, out_prod_mr, out_conv_se, out_head, out_filter, out_small,
    win, inv_cols, dot_cols,
):
    @pl.when(pl.program_id(0) == 0)
    def _():
        sums = jnp.sum(stats[...], axis=0)
        inv = lax.rsqrt(sums[0:1] / D + 1e-06)
        dot = inv * inv * inv * sums[1:2] / D
        inv_cols[...] = jnp.broadcast_to(inv, (128, 128)).T
        dot_cols[...] = jnp.broadcast_to(dot, (128, 128)).T

    reps = mixed.shape[1] // 128
    inv = jnp.concatenate([inv_cols[...]] * reps, axis=1)
    dot = jnp.concatenate([dot_cols[...]] * reps, axis=1)
    m = mixed[...]
    gp = prod[...]
    g = gain[...].astype(F32)
    k = key_mr[...].astype(F32)
    scaled_mixed = m * inv
    normed = (scaled_mixed * g).astype(BF16).astype(F32)
    p = (k * normed).astype(BF16)
    out_prod_mr[...] = p
    out_key_mr[...] = (gp * normed).astype(BF16)
    grad = correlated(back[...], to_spectrum(half[...], p), spectrum[...])
    for b in range(reps):
        tile = grad[:, 128 * b : 128 * b + 128].reshape(out_filter.shape[0], 8, 128)
        out_filter[:, b] = tile.astype(BF16)
    grad_normed = gp * k
    gain_row = jnp.sum(grad_normed * scaled_mixed, axis=0, keepdims=True)
    grad_mixed = inv * (grad_normed * g) - m * dot
    out_query_se[...] = (grad_mixed * conv[...]).astype(BF16)
    gcs = (grad_mixed * query_se[...].astype(F32)).astype(BF16)
    out_conv_se[...] = gcs
    out_head[...] = gcs[:HALO]
    gcs = gcs.astype(F32)
    se_window(win, rim, key_se, value)
    taps = out_small.shape[0] - 1
    rows = [
        jnp.sum(gcs * win[HALO - j : HALO - j + 128], axis=0, keepdims=True) for j in range(taps)
    ]
    out_small[...] = jnp.concatenate(rows + [gain_row], axis=0)


def last_kernel(
    prod_mr, rim_mr, out_grad, kernel, conv_se, rim_se, taps_se, value, key_se, whole, back,
    out_query_mr, out_key_se, out_value, win,
):
    signal = to_spectrum(whole[...], rim_mr[...], prod_mr[...])
    conv = convolved(back[...], kernel[...], signal)
    out_query_mr[...] = (out_grad[...].astype(F32) * conv).astype(BF16)
    win[0:128] = conv_se[...].astype(F32)
    win[128:] = rim_se[...].astype(F32)
    f = taps_se[...].astype(F32)
    total = f[0:1] * win[0:128]
    for j in range(1, f.shape[0]):
        total = total + f[j : j + 1] * win[j : j + 128]
    out_key_se[...] = (total * value[...].astype(F32)).astype(BF16)
    out_value[...] = (total * key_se[...].astype(F32)).astype(BF16)


def plane_kernel(part, other, rim_mr, rim_se, out):
    del rim_mr, rim_se
    out[...] = (part[...] + other[...]).astype(BF16)


def unpack_kernel(tiles, small, out_mr, out_se, out_gain):
    taps = out_se.shape[0]
    for b in range(small.shape[0]):
        lanes = slice(128 * b, 128 * b + 128)
        out_mr[:, lanes] = tiles[:, b].astype(F32).reshape(out_mr.shape[0], 128)
        out_se[:, lanes] = small[b, :taps]
        out_gain[:, lanes] = small[b, taps:]


def wide(rows):
    return pl.BlockSpec((rows, WIDTH), lambda i: (0, i))


def fixed(*shape):
    return pl.BlockSpec(shape, lambda i: (0,) * len(shape))


def call(kernel, cols, in_specs, out_specs, out_shape, scratch, flops, moved):
    return pl.pallas_call(
        kernel,
        grid=(cols // WIDTH,),
        in_specs=in_specs,
        out_specs=out_specs,
        out_shape=[jax.ShapeDtypeStruct(s, d) for s, d in out_shape],
        scratch_shapes=scratch,
        compiler_params=pltpu.CompilerParams(vmem_limit_bytes=40 * 1024 * 1024),
        cost_estimate=pl.CostEstimate(flops=flops, bytes_accessed=moved, transcendentals=0),
    )


def shifted(block, axis, distance):
    devices = range(lax.axis_size(axis))
    route = [(i - distance, i) for i in devices if i - distance in devices]
    return lax.ppermute(block, axis, route)


def filter_totals(tiles, small, rims):
    n = lax.axis_size("ctx")
    plane = n // 2
    planes = [list(range(plane)), list(range(plane, n))]
    cols = small.shape[1]
    rows = small.reshape(8, -1, 128).transpose(1, 0, 2).reshape(plane, 1, 1, 128).astype(BF16)
    rows = jnp.pad(rows, ((0, 0), (0, 0), (0, 1), (0, 0)))
    packed = jnp.concatenate([tiles.reshape(plane, 8, 2, 128), rows], axis=1)
    got = lax.all_to_all(packed, "ctx", 0, 0, axis_index_groups=planes, tiled=True)
    part = jnp.sum(got.astype(F32), axis=0)
    other = lax.ppermute(part, "ctx", [(i, (i + plane) % n) for i in range(n)])
    total = pl.pallas_call(
        plane_kernel,
        out_shape=jax.ShapeDtypeStruct(part.shape, BF16),
    )(part, other, *[rim[:HALO, :128] for rim in rims])
    spread = jnp.broadcast_to(total[None], (plane,) + total.shape)
    back = lax.all_to_all(spread, "ctx", 0, 0, axis_index_groups=planes, tiled=True)
    mr_shape, se_shape = (tiles.shape[0] * 8, cols), (small.shape[0] - 1, cols)
    return pl.pallas_call(
        unpack_kernel,
        out_shape=[jax.ShapeDtypeStruct(shape, F32) for shape in (mr_shape, se_shape, (1, cols))],
    )(back[:, :8].reshape(tiles.shape), back[:, 8, 0].astype(F32).reshape(-1, 8, 128))


def shards(
    value_path, key_se, query_se, key_mr, query_mr, out_grad, norm_gain, filter_se, filter_mr
):
    tokens, cols = value_path.shape
    se_taps = filter_se.shape[0]
    full = (tokens, cols)
    whole, half, later, back_first, back_last = transforms()
    gain = norm_gain.reshape(1, cols)
    tail = (key_se[-HALO:].astype(F32) * value_path[-HALO:].astype(F32)).astype(BF16)
    grad_conv_mr = (out_grad.astype(F32) * query_mr.astype(F32)).astype(BF16)
    rim_se = shifted(tail, "ctx", 1)
    rim_grad_mr = shifted(grad_conv_mr, "ctx", -1)
    half_spec, back_spec = fixed(*half.shape), fixed(*back_first.shape)
    spectral = (2 * tokens, cols)
    kernel_mr, near = call(
        spectra_kernel,
        cols,
        [wide(tokens)] * 2 + [half_spec],
        [wide(2 * tokens)] * 2,
        [(spectral, F32)] * 2,
        [],
        2000 * tokens * cols,
        20 * tokens * cols,
    )(grad_conv_mr, filter_mr, half)
    conv_se, mixed_se, square = call(
        se_kernel,
        cols,
        [wide(tokens)] * 3 + [wide(HALO), wide(se_taps)],
        [wide(tokens), wide(tokens), fixed(tokens, 128)],
        [(full, F32), (full, F32), ((tokens, 128), F32)],
        [pltpu.VMEM((tokens + HALO, WIDTH), F32)],
        18 * tokens * cols,
        14 * tokens * cols,
    )(key_se, value_path, query_se, rim_se, filter_se)
    grad_prod_mr, spectrum, stats = call(
        dot_kernel,
        cols,
        [wide(2 * tokens), wide(tokens), wide(2 * tokens), wide(tokens), wide(1), wide(tokens)]
        + [fixed(tokens, 128), half_spec, back_spec],
        [wide(tokens), wide(2 * tokens), fixed(8, 8, 128)],
        [(full, F32), (spectral, F32), ((8, 8, 128), F32)],
        [pltpu.VMEM((tokens, 128), F32)],
        3000 * tokens * cols,
        24 * tokens * cols,
    )(near, rim_grad_mr, kernel_mr, key_mr, gain, mixed_se, square, later, back_first)
    stats = lax.all_to_all(stats, "tp", 0, 0, tiled=True)
    groups = filter_mr.shape[0] // 8
    (
        grad_query_se, grad_key_mr, prod_mr, grad_conv_se, head, tiles, small
    ) = call(
        main_kernel,
        cols,
        [fixed(8, 8, 128)] + [wide(tokens)] * 3 + [wide(2 * tokens)] + [wide(tokens)] * 4
        + [wide(HALO), wide(1), half_spec, back_spec],
        [wide(tokens)] * 4
        + [wide(HALO), pl.BlockSpec((groups, WIDTH // 128, 8, 128), lambda i: (0, i, 0, 0))]
        + [wide(se_taps + 1)],
        [(full, BF16)] * 4
        + [((HALO, cols), BF16), ((groups, cols // 128, 8, 128), BF16), ((se_taps + 1, cols), F32)],
        [pltpu.VMEM((tokens + HALO, WIDTH), F32)] + [pltpu.VMEM((tokens, 128), F32)] * 2,
        2000 * tokens * cols,
        40 * tokens * cols,
    )(
        stats, mixed_se, conv_se, grad_prod_mr, spectrum, key_mr, query_se, key_se, value_path,
        rim_se, gain, half, back_first,
    )
    rim_mr = shifted(prod_mr, "ctx", 1)
    rim_grad_se = shifted(head, "ctx", -1)
    grad_filter_mr, grad_filter_se, grad_gain = filter_totals(tiles, small, (rim_mr, rim_grad_se))
    grad_query_mr, grad_key_se, grad_value = call(
        last_kernel,
        cols,
        [wide(tokens)] * 3 + [wide(2 * tokens), wide(tokens), wide(HALO), wide(se_taps)]
        + [wide(tokens)] * 2 + [fixed(*whole.shape), back_spec],
        [wide(tokens)] * 3,
        [(full, BF16)] * 3,
        [pltpu.VMEM((tokens + HALO, WIDTH), F32)],
        3000 * tokens * cols,
        20 * tokens * cols,
    )(
        prod_mr, rim_mr, out_grad, kernel_mr, grad_conv_se, rim_grad_se, filter_se, value_path,
        key_se, whole, back_last,
    )
    return (
        grad_value,
        grad_query_se,
        grad_key_se,
        grad_query_mr,
        grad_key_mr,
        grad_filter_se,
        grad_filter_mr,
        grad_gain.reshape(cols),
    )


def solution(mesh):
    spread = P("ctx", "tp")
    return jax.shard_map(
        shards,
        mesh=mesh,
        in_specs=(spread,) * 6 + (P("tp"), P(None, "tp"), P(None, "tp")),
        out_specs=(spread,) * 5 + (P(None, "tp"), P(None, "tp"), P("tp")),
        check_vma=False,
    )
```

```python
import jax
import jax.numpy as jnp
import numpy as np
from jax import lax
from jax.experimental import pallas as pl
from jax.experimental.pallas import tpu as pltpu
from jax.sharding import PartitionSpec as P

D = 8192
WIDTH = 1024
HALO = 16
F32 = jnp.float32
BF16 = jnp.bfloat16


def split(matrix):
    high = matrix.astype(jnp.bfloat16)
    low = (matrix - high.astype(np.float64)).astype(jnp.bfloat16)
    return high, low


def transforms():
    phase = 2 * np.pi * np.outer(np.arange(128) + 0.5, np.arange(256)) / 256
    forward = np.concatenate([np.cos(phase), -np.sin(phase)], axis=0)
    inverse = forward.T / 128
    f_high, f_low = split(forward)
    i_high, i_low = split(inverse)
    whole = np.concatenate([f_high, f_low], axis=1)
    half = np.concatenate([f_high[:, :128], f_low[:, :128]], axis=1)
    later = np.concatenate([f_high[:, 128:], f_low[:, 128:]], axis=1)
    back = np.concatenate([i_high, i_high, i_low], axis=1)
    return [jnp.asarray(m) for m in (whole, half, later, back[:128], back[128:])]


def to_spectrum(matrix, *rows):
    return jnp.dot(matrix, jnp.concatenate(rows + rows, axis=0), preferred_element_type=F32)


def from_spectrum(matrix, re, im):
    both = jnp.concatenate([re, im], axis=0)
    high = both.astype(BF16)
    low = (both - high.astype(F32)).astype(BF16)
    return jnp.dot(matrix, jnp.concatenate([high, low, high], axis=0), preferred_element_type=F32)


def correlated(matrix, kernel, signal):
    k_re, k_im = kernel[:128], kernel[128:]
    s_re, s_im = signal[:128], signal[128:]
    return from_spectrum(matrix, k_re * s_re + k_im * s_im, k_re * s_im - k_im * s_re)


def convolved(matrix, kernel, signal):
    k_re, k_im = kernel[:128], kernel[128:]
    s_re, s_im = signal[:128], signal[128:]
    return from_spectrum(matrix, k_re * s_re - k_im * s_im, k_re * s_im + k_im * s_re)


def lane_blocks(value):
    return sum(value[:, i : i + 128] for i in range(0, value.shape[1], 128))


def se_window(win, rim, key, value):
    prod = (key[...].astype(F32) * value[...].astype(F32)).astype(BF16)
    win[0:HALO] = rim[...].astype(F32)
    win[HALO:] = prod.astype(F32)


def spectra_kernel(grad, taps, half, kernel, near):
    kernel[...] = to_spectrum(half[...], taps[...])
    near[...] = to_spectrum(half[...], grad[...])


def se_kernel(key, value, query, rim, taps, conv, mixed, square, win):
    se_window(win, rim, key, value)
    f = taps[...].astype(F32)
    total = f[0:1] * win[HALO : HALO + 128]
    for j in range(1, f.shape[0]):
        total = total + f[j : j + 1] * win[HALO - j : HALO - j + 128]
    conv[...] = total
    m = query[...].astype(F32) * total
    mixed[...] = m

    @pl.when(pl.program_id(0) == 0)
    def _():
        square[...] = jnp.zeros_like(square)

    square[...] += lane_blocks(m * m)


def dot_kernel(
    near, rim, kernel, key, gain, mixed, square, later, back, prod, spectrum, stats, acc
):
    signal = near[...] + to_spectrum(later[...], rim[...])
    spectrum[...] = signal
    gp = correlated(back[...], kernel[...], signal)
    prod[...] = gp
    scaled = gp * key[...].astype(F32) * gain[...].astype(F32)

    @pl.when(pl.program_id(0) == 0)
    def _():
        acc[...] = jnp.zeros_like(acc)

    acc[...] += lane_blocks(scaled * mixed[...])

    @pl.when(pl.program_id(0) == pl.num_programs(0) - 1)
    def _():
        squares = jnp.sum(square[...].T, axis=0, keepdims=True)
        dots = jnp.sum(acc[...].T, axis=0, keepdims=True)
        row = lax.broadcasted_iota(jnp.int32, (8, 128), 0)
        both = jnp.where(row == 0, squares, jnp.where(row == 1, dots, 0.0))
        stats[...] = jnp.broadcast_to(both[None], stats.shape)


def main_kernel(
    stats, mixed, conv, prod, spectrum, key_mr, query_se, key_se, value, rim, gain, half, back,
    out_query_se, out_key_mr, out_prod_mr, out_conv_se, out_head, out_filter, out_small,
    win, inv_cols, dot_cols,
):
    @pl.when(pl.program_id(0) == 0)
    def _():
        sums = jnp.sum(stats[...], axis=0)
        inv = lax.rsqrt(sums[0:1] / D + 1e-06)
        dot = inv * inv * inv * sums[1:2] / D
        inv_cols[...] = jnp.broadcast_to(inv, (128, 128)).T
        dot_cols[...] = jnp.broadcast_to(dot, (128, 128)).T

    reps = mixed.shape[1] // 128
    inv = jnp.concatenate([inv_cols[...]] * reps, axis=1)
    dot = jnp.concatenate([dot_cols[...]] * reps, axis=1)
    m = mixed[...]
    gp = prod[...]
    g = gain[...].astype(F32)
    k = key_mr[...].astype(F32)
    scaled_mixed = m * inv
    normed = (scaled_mixed * g).astype(BF16).astype(F32)
    p = (k * normed).astype(BF16)
    out_prod_mr[...] = p
    out_key_mr[...] = (gp * normed).astype(BF16)
    grad = correlated(back[...], to_spectrum(half[...], p), spectrum[...])
    for b in range(reps):
        tile = grad[:, 128 * b : 128 * b + 128].reshape(out_filter.shape[0], 8, 128)
        out_filter[:, b] = tile.astype(BF16)
    grad_normed = gp * k
    gain_row = jnp.sum(grad_normed * scaled_mixed, axis=0, keepdims=True)
    grad_mixed = inv * (grad_normed * g) - m * dot
    out_query_se[...] = (grad_mixed * conv[...]).astype(BF16)
    gcs = (grad_mixed * query_se[...].astype(F32)).astype(BF16)
    out_conv_se[...] = gcs
    out_head[...] = gcs[:HALO]
    gcs = gcs.astype(F32)
    se_window(win, rim, key_se, value)
    taps = out_small.shape[0] - 1
    rows = [
        jnp.sum(gcs * win[HALO - j : HALO - j + 128], axis=0, keepdims=True) for j in range(taps)
    ]
    out_small[...] = jnp.concatenate(rows + [gain_row], axis=0)


def last_kernel(
    prod_mr, rim_mr, out_grad, kernel, conv_se, rim_se, taps_se, value, key_se, whole, back,
    out_query_mr, out_key_se, out_value, win,
):
    signal = to_spectrum(whole[...], rim_mr[...], prod_mr[...])
    conv = convolved(back[...], kernel[...], signal)
    out_query_mr[...] = (out_grad[...].astype(F32) * conv).astype(BF16)
    win[0:128] = conv_se[...].astype(F32)
    win[128:] = rim_se[...].astype(F32)
    f = taps_se[...].astype(F32)
    total = f[0:1] * win[0:128]
    for j in range(1, f.shape[0]):
        total = total + f[j : j + 1] * win[j : j + 128]
    out_key_se[...] = (total * value[...].astype(F32)).astype(BF16)
    out_value[...] = (total * key_se[...].astype(F32)).astype(BF16)


def plane_kernel(part, other, rim_mr, rim_se, out):
    del rim_mr, rim_se
    out[...] = (part[...] + other[...]).astype(BF16)


def unpack_kernel(tiles, small, out_mr, out_se, out_gain):
    taps = out_se.shape[0]
    for b in range(small.shape[0]):
        lanes = slice(128 * b, 128 * b + 128)
        out_mr[:, lanes] = tiles[:, b].astype(F32).reshape(out_mr.shape[0], 128)
        out_se[:, lanes] = small[b, :taps]
        out_gain[:, lanes] = small[b, taps:]


def wide(rows):
    return pl.BlockSpec((rows, WIDTH), lambda i: (0, i))


def fixed(*shape):
    return pl.BlockSpec(shape, lambda i: (0,) * len(shape))


def call(kernel, cols, in_specs, out_specs, out_shape, scratch, flops, moved):
    return pl.pallas_call(
        kernel,
        grid=(cols // WIDTH,),
        in_specs=in_specs,
        out_specs=out_specs,
        out_shape=[jax.ShapeDtypeStruct(s, d) for s, d in out_shape],
        scratch_shapes=scratch,
        compiler_params=pltpu.CompilerParams(vmem_limit_bytes=40 * 1024 * 1024),
        cost_estimate=pl.CostEstimate(flops=flops, bytes_accessed=moved, transcendentals=0),
    )


def shifted(block, axis, distance):
    devices = range(lax.axis_size(axis))
    route = [(i - distance, i) for i in devices if i - distance in devices]
    return lax.ppermute(block, axis, route)


def filter_totals(tiles, small, rims):
    n = lax.axis_size("ctx")
    plane = n // 2
    planes = [list(range(plane)), list(range(plane, n))]
    cols = small.shape[1]
    rows = small.reshape(8, -1, 128).transpose(1, 0, 2).reshape(plane, 1, 1, 128).astype(BF16)
    rows = jnp.pad(rows, ((0, 0), (0, 0), (0, 1), (0, 0)))
    packed = jnp.concatenate([tiles.reshape(plane, 8, 2, 128), rows], axis=1)
    got = lax.all_to_all(packed, "ctx", 0, 0, axis_index_groups=planes, tiled=True)
    part = jnp.sum(got.astype(F32), axis=0)
    other = lax.ppermute(part, "ctx", [(i, (i + plane) % n) for i in range(n)])
    total = pl.pallas_call(
        plane_kernel,
        out_shape=jax.ShapeDtypeStruct(part.shape, BF16),
        compiler_params=pltpu.CompilerParams(vmem_limit_bytes=2 * 1024 * 1024),
    )(part, other, *[rim[:HALO, :128] for rim in rims])
    spread = jnp.broadcast_to(total[None], (plane,) + total.shape)
    back = lax.all_to_all(spread, "ctx", 0, 0, axis_index_groups=planes, tiled=True)
    mr_shape, se_shape = (tiles.shape[0] * 8, cols), (small.shape[0] - 1, cols)
    return pl.pallas_call(
        unpack_kernel,
        out_shape=[jax.ShapeDtypeStruct(shape, F32) for shape in (mr_shape, se_shape, (1, cols))],
        compiler_params=pltpu.CompilerParams(vmem_limit_bytes=6 * 1024 * 1024),
    )(back[:, :8].reshape(tiles.shape), back[:, 8, 0].astype(F32).reshape(-1, 8, 128))


def shards(
    value_path, key_se, query_se, key_mr, query_mr, out_grad, norm_gain, filter_se, filter_mr
):
    tokens, cols = value_path.shape
    se_taps = filter_se.shape[0]
    full = (tokens, cols)
    whole, half, later, back_first, back_last = transforms()
    gain = norm_gain.reshape(1, cols)
    tail = (key_se[-HALO:].astype(F32) * value_path[-HALO:].astype(F32)).astype(BF16)
    grad_conv_mr = (out_grad.astype(F32) * query_mr.astype(F32)).astype(BF16)
    rim_se = shifted(tail, "ctx", 1)
    rim_grad_mr = shifted(grad_conv_mr, "ctx", -1)
    half_spec, back_spec = fixed(*half.shape), fixed(*back_first.shape)
    spectral = (2 * tokens, cols)
    kernel_mr, near = call(
        spectra_kernel,
        cols,
        [wide(tokens)] * 2 + [half_spec],
        [wide(2 * tokens)] * 2,
        [(spectral, F32)] * 2,
        [],
        2000 * tokens * cols,
        20 * tokens * cols,
    )(grad_conv_mr, filter_mr, half)
    conv_se, mixed_se, square = call(
        se_kernel,
        cols,
        [wide(tokens)] * 3 + [wide(HALO), wide(se_taps)],
        [wide(tokens), wide(tokens), fixed(tokens, 128)],
        [(full, F32), (full, F32), ((tokens, 128), F32)],
        [pltpu.VMEM((tokens + HALO, WIDTH), F32)],
        18 * tokens * cols,
        14 * tokens * cols,
    )(key_se, value_path, query_se, rim_se, filter_se)
    grad_prod_mr, spectrum, stats = call(
        dot_kernel,
        cols,
        [wide(2 * tokens), wide(tokens), wide(2 * tokens), wide(tokens), wide(1), wide(tokens)]
        + [fixed(tokens, 128), half_spec, back_spec],
        [wide(tokens), wide(2 * tokens), fixed(8, 8, 128)],
        [(full, F32), (spectral, F32), ((8, 8, 128), F32)],
        [pltpu.VMEM((tokens, 128), F32)],
        3000 * tokens * cols,
        24 * tokens * cols,
    )(near, rim_grad_mr, kernel_mr, key_mr, gain, mixed_se, square, later, back_first)
    stats = lax.all_to_all(stats, "tp", 0, 0, tiled=True)
    groups = filter_mr.shape[0] // 8
    (
        grad_query_se, grad_key_mr, prod_mr, grad_conv_se, head, tiles, small
    ) = call(
        main_kernel,
        cols,
        [fixed(8, 8, 128)] + [wide(tokens)] * 3 + [wide(2 * tokens)] + [wide(tokens)] * 4
        + [wide(HALO), wide(1), half_spec, back_spec],
        [wide(tokens)] * 4
        + [wide(HALO), pl.BlockSpec((groups, WIDTH // 128, 8, 128), lambda i: (0, i, 0, 0))]
        + [wide(se_taps + 1)],
        [(full, BF16)] * 4
        + [((HALO, cols), BF16), ((groups, cols // 128, 8, 128), BF16), ((se_taps + 1, cols), F32)],
        [pltpu.VMEM((tokens + HALO, WIDTH), F32)] + [pltpu.VMEM((tokens, 128), F32)] * 2,
        2000 * tokens * cols,
        40 * tokens * cols,
    )(
        stats, mixed_se, conv_se, grad_prod_mr, spectrum, key_mr, query_se, key_se, value_path,
        rim_se, gain, half, back_first,
    )
    rim_mr = shifted(prod_mr, "ctx", 1)
    rim_grad_se = shifted(head, "ctx", -1)
    grad_filter_mr, grad_filter_se, grad_gain = filter_totals(tiles, small, (rim_mr, rim_grad_se))
    grad_query_mr, grad_key_se, grad_value = call(
        last_kernel,
        cols,
        [wide(tokens)] * 3 + [wide(2 * tokens), wide(tokens), wide(HALO), wide(se_taps)]
        + [wide(tokens)] * 2 + [fixed(*whole.shape), back_spec],
        [wide(tokens)] * 3,
        [(full, BF16)] * 3,
        [pltpu.VMEM((tokens + HALO, WIDTH), F32)],
        3000 * tokens * cols,
        20 * tokens * cols,
    )(
        prod_mr, rim_mr, out_grad, kernel_mr, grad_conv_se, rim_grad_se, filter_se, value_path,
        key_se, whole, back_last,
    )
    return (
        grad_value,
        grad_query_se,
        grad_key_se,
        grad_query_mr,
        grad_key_mr,
        grad_filter_se,
        grad_filter_mr,
        grad_gain.reshape(cols),
    )


def solution(mesh):
    spread = P("ctx", "tp")
    return jax.shard_map(
        shards,
        mesh=mesh,
        in_specs=(spread,) * 6 + (P("tp"), P(None, "tp"), P(None, "tp")),
        out_specs=(spread,) * 5 + (P(None, "tp"), P(None, "tp"), P("tp")),
        check_vma=False,
    )
```
